512 devices in a mesh: head: 16 (over z_hi, x, core), ctx: 32 (over z_lo, y).
Axes of the slice: x: 4, y: 4, z: 16 (z_hi: 2, z_lo: 8; z = z_hi * 8 + z_lo), core: 2. Of those that a mesh axis runs over, the one named last changes fastest.
Arguments:
- queries: bfloat16 [4096, 128, 128], P('ctx', 'head'), may hold values from -8 to 8
- keys: bfloat16 [4096, 1024], P('ctx', 'head'), may hold values from -8 to 8
- values: bfloat16 [4096, 1024], P('ctx', 'head'), may hold values from -6 to 6
- stretch_order: int32 [32, 2], replicated, may hold values from 0 to 63, as said below
Outputs:
- attended: bfloat16 [4096, 128, 128], P('ctx', 'head')
The draws below stay inside these ranges and needn't reach their ends.
Inputs may be any that keep to these rules, and one draw needn't show every extreme that they name: `stretch_order`: every stretch 0 to 63 stands exactly once in the table, and the two stretches of a row add up to 63.
All inputs are finite; a program needn't handle non-finite values.
Results may differ from the reference program's by a relative error of at most 0.035.
Values may be sent and summed in bfloat16 or wider, within the bound.
A program may use at most 64 MiB of HBM per device.

```python
import jax
import jax.numpy as jnp
from jax import lax

DH = 128
GROUP = 16
TOK_DEV = 128
STRETCH = 64
NCHUNK = 64
SEQ = 4096
HQ = 128
KVH = 8
N_CTX = 32


def draw_queries(key, part):
    key = jax.random.fold_in(key, 11)
    result = jnp.clip(1.7 * jax.random.normal(key, (SEQ, HQ, DH), jnp.float32), -8.0, 8.0)
    return result.astype(jnp.bfloat16)


def draw_keys(key, part):
    key = jax.random.fold_in(key, 23)
    result = jnp.clip(1.7 * jax.random.normal(key, (SEQ, KVH * DH), jnp.float32), -8.0, 8.0)
    return result.astype(jnp.bfloat16)


def draw_stretch_order(key, part):
    key = jax.random.fold_in(key, 5)
    first, second = jax.random.split(key)
    devices = NCHUNK // 2
    pairs = jax.random.permutation(first, devices).astype(jnp.int32)
    flips = jax.random.randint(second, (devices,), 0, 2).astype(jnp.int32)
    leading = jnp.where(flips == 1, NCHUNK - 1 - pairs, pairs).astype(jnp.int32)
    trailing = (NCHUNK - 1 - leading).astype(jnp.int32)
    return jnp.stack([leading, trailing], axis=1)


def levels(rng, extent, cuts, low, top_value):
    def one(position, blocks):
        steps = jax.random.uniform(jax.random.fold_in(jax.random.fold_in(rng, 6), position), (blocks,), jnp.float32, low / len(cuts), top_value / len(cuts))
        return jnp.repeat(jnp.exp(steps), extent[position] // blocks).reshape((-1,) + (1,) * (len(extent) - position - 1))

    factor_of = one(*cuts[0])
    for cut in cuts[1:]:
        factor_of = factor_of * one(*cut)
    return factor_of


def centred(own_key, shape, width, most, cuts=(), kind=jnp.bfloat16):
    array = width * jax.random.normal(own_key, shape, jnp.float32)
    if cuts:
        array = array * levels(own_key, shape, cuts, -0.22, 0.18)
    return jnp.clip(array, -most, most).astype(kind)


def setup_inputs(seed: int = 0) -> dict:
    splits = jax.random.split(jax.random.key(seed), 5)
    return {
        "queries": draw_queries(jax.random.fold_in(splits[4], 71), 0),
        "keys": draw_keys(jax.random.fold_in(splits[4], 71), 0),
        "values": centred(splits[2], (SEQ, KVH * DH), 1.0, 6.0, ((0, 32), (1, 16))),
        "stretch_order": draw_stretch_order(jax.random.fold_in(splits[4], 71), 0),
    }


def reference(queries, keys, values, stretch_order):
    seq_len = queries.shape[0]
    table = stretch_order.reshape(-1)
    rows = jnp.arange(seq_len, dtype=jnp.int32)
    positions = (table[rows // STRETCH] * STRETCH + rows % STRETCH).astype(jnp.int32)
    key_pos = positions.reshape(N_CTX, TOK_DEV)
    key_heads = keys.reshape(N_CTX, TOK_DEV, KVH, DH).astype(jnp.float32)
    value_heads = values.reshape(N_CTX, TOK_DEV, KVH, DH).astype(jnp.float32)
    query_blocks = queries.reshape(N_CTX, TOK_DEV, KVH, GROUP, DH)
    scale = DH ** -0.5

    def one_block(args):
        block, query_pos = args
        scores = jnp.einsum("tgqd,nsgd->ntgqs", block.astype(jnp.float32), key_heads) * scale
        visible = key_pos[:, None, None, None, :] <= query_pos[None, :, None, None, None]
        scores = jnp.where(visible, scores, jnp.float32(-1e30))
        top = jnp.max(scores, axis=-1)
        weights = jnp.exp(scores - top[..., None])
        total = jnp.sum(weights, axis=-1)
        rounded = lax.optimization_barrier(weights.astype(jnp.bfloat16)).astype(jnp.float32)
        mixed = jnp.einsum("ntgqs,nsgd->ntgqd", rounded, value_heads) / total[..., None]
        mixed = lax.optimization_barrier(mixed.astype(jnp.bfloat16)).astype(jnp.float32)
        lse = top + jnp.log(total)
        biggest = jnp.max(lse, axis=0)
        share = jnp.exp(lse - biggest[None])
        merged = jnp.sum(share[..., None] * mixed, axis=0) / jnp.sum(share, axis=0)[..., None]
        return merged.astype(jnp.bfloat16)

    merged_all = lax.map(one_block, (query_blocks, key_pos))
    return merged_all.reshape(seq_len, KVH * GROUP, DH)
```

```python
import functools
import math

import jax
import jax.numpy as jnp
from jax import lax
from jax.experimental import pallas as pl
from jax.experimental.pallas import tpu as pltpu
from jax.sharding import PartitionSpec as P

MESH = pl.DeviceIdType.MESH
NEG = -1e30


def along_y(s):
    return [("send", s, 1), ("send", s, 3), ("send", s, 2)]


def along_z(s):
    return [("send", s, 12), ("send", s, 8), ("send", s, 4)]


def swap(g):
    return [("swap", 4 * g, 4)]


def attend(g):
    return [("attend", g)]


PROGRAM = (
    [("send", 0, 16)] + along_z(0) + along_y(0)
    + along_y(4) + along_y(8) + along_y(12) + swap(0)
    + along_z(16) + along_y(16) + attend(0)
    + swap(1) + swap(2) + swap(3)
    + attend(1)
    + along_y(20) + along_y(24) + along_y(28)
    + attend(2) + attend(3)
    + swap(4) + attend(4) + swap(5) + swap(6) + attend(5) + swap(7) + attend(6) + attend(7)
)
SENDS = sum(op[0] == "send" for op in PROGRAM)
SWAPS = sum(op[0] == "swap" for op in PROGRAM)


def kernel(
    q_hbm, k_ref, v_ref, table, out_ref,
    q_raw, q_wide, mine, theirs, bias, top, total, acc,
    q_sem, send_sem, recv_sem, swap_send, swap_recv,
):
    h = lax.axis_index("head")
    c = lax.axis_index("ctx")
    tokens = k_ref.shape[0]
    half = k_ref.shape[1]
    width = 2 * half
    rows = q_raw.shape[0]
    heads = rows // tokens
    stretch = tokens // 2
    upper = h % 2 == 1
    keys = 4 * tokens
    factor = width ** (-0.5) * math.log2(math.e)

    q_copy = pltpu.make_async_copy(q_hbm, q_raw, q_sem)
    q_copy.start()
    jumps = sorted({op[2] for op in PROGRAM if op[0] == "send"}, reverse=True)
    barrier = pltpu.get_barrier_semaphore()
    for k in jumps:
        pl.semaphore_signal(barrier, inc=1, device_id=(h, c ^ k), device_id_type=MESH)
    pl.semaphore_signal(barrier, inc=1, device_id=(h ^ 1, c), device_id_type=MESH)

    kk, vv = k_ref[...], v_ref[...]
    mine[0] = jnp.where(
        upper, jnp.concatenate([kk, vv], axis=1), jnp.concatenate([vv, kk], axis=1)
    )
    pl.semaphore_wait(barrier, len(jumps) + 1)

    def remote(s, k, i):
        return pltpu.make_async_remote_copy(
            src_ref=mine.at[s], dst_ref=mine.at[s ^ k],
            send_sem=send_sem.at[i], recv_sem=recv_sem.at[s ^ k],
            device_id=(h, c ^ k), device_id_type=MESH,
        )

    def across(s, n, i):
        part = pl.ds(s, n)
        return pltpu.make_async_remote_copy(
            src_ref=mine.at[part], dst_ref=theirs.at[part],
            send_sem=swap_send.at[i], recv_sem=swap_recv.at[i],
            device_id=(h ^ 1, c), device_id_type=MESH,
        )

    def prepare():
        q_copy.wait()
        lane = lax.broadcasted_iota(jnp.int32, (1, width), 1)
        low = lane < half
        raw = q_raw[...].astype(jnp.float32)
        rolled = jnp.concatenate([raw[:, half:], raw[:, :half]], axis=1)
        left = jnp.where(low, rolled, 0.0)
        right = jnp.where(low, 0.0, rolled)
        q_wide[:, :width] = jnp.where(upper, left, right).astype(jnp.bfloat16)
        q_wide[:, width:] = jnp.where(upper, right, left).astype(jnp.bfloat16)
        for s in range(mine.shape[0]):
            b = c ^ s
            held = jnp.where(low, table[b, 0], table[b, 1])
            for a in range(2):
                bias[a, s // 4 : s // 4 + 1, (s % 4) * tokens : (s % 4 + 1) * tokens] = jnp.where(
                    held < table[c, a], 0.0, NEG
                )

    def group(g):
        part = pl.ds(4 * g, 4)
        return jnp.concatenate(
            [mine[part].reshape(keys, width), theirs[part].reshape(keys, width)], axis=1
        )

    def step(g, a):
        span = pl.ds(a * (rows // 2), rows // 2)
        kv = group(g)
        scores = lax.dot_general(
            q_wide[span, :], kv, (((1,), (1,)), ((), ())), preferred_element_type=jnp.float32
        )
        shut = bias[pl.ds(a, 1), g : g + 1, :].reshape(1, keys)
        if g == 0:
            lane = lax.broadcasted_iota(jnp.int32, (1, tokens), 1)
            held = jnp.where(
                lane < stretch, table[c, 0] * stretch + lane, table[c, 1] * stretch + lane - stretch
            )
            row = lax.broadcasted_iota(jnp.int32, (rows // 2, 1), 0) // heads
            seen = held <= table[c, a] * stretch + row
            own = jnp.where(seen, scores[:, :tokens], NEG)
            scores = jnp.concatenate([own, scores[:, tokens:] + shut[:, tokens:]], axis=1)
            new_top = jnp.max(scores, axis=1, keepdims=True)
        else:
            scores = scores + shut
            old_top = top[span, :1]
            new_top = jnp.maximum(old_top, jnp.max(scores, axis=1, keepdims=True))
        weights = jnp.exp2((scores - new_top) * factor)
        partial = (
            weights[:, :tokens] + weights[:, tokens : 2 * tokens]
            + weights[:, 2 * tokens : 3 * tokens] + weights[:, 3 * tokens :]
        )
        mixed = jnp.dot(weights.astype(jnp.bfloat16), kv, preferred_element_type=jnp.float32)
        if g == 0:
            total[span, :] = partial
            acc[span, :] = mixed
        else:
            fade = jnp.exp2((old_top - new_top) * factor)
            total[span, :] = total[span, :] * fade + partial
            acc[span, :] = acc[span, :] * fade + mixed
        top[span, :] = jnp.broadcast_to(new_top, (rows // 2, tokens))

    here = {0}

    def arrived(s):
        if s not in here:
            here.add(s)
            remote(s ^ 1, 1, 0).wait_recv()

    sent, swapped, swap_of = [], [], {}
    first = True
    for op in PROGRAM:
        if op[0] == "send":
            arrived(op[1])
            sent.append(remote(op[1], op[2], len(sent)))
            sent[-1].start()
            if first and len(sent) == len(jumps):
                prepare()
                first = False
        elif op[0] == "swap":
            for s in range(op[1], op[1] + op[2]):
                arrived(s)
                swap_of[s] = len(swapped)
            swapped.append(across(op[1], op[2], len(swapped)))
            swapped[-1].start()
        else:
            g = op[1]
            swapped[swap_of[4 * g]].wait_recv()

            def body(a, carry, g=g):
                step(g, a)
                return carry

            lax.fori_loop(0, 2, body, 0)

    whole = jnp.sum(total[...], axis=1, keepdims=True)
    lane = lax.broadcasted_iota(jnp.int32, (1, width), 1)
    pick = (lane < half) != upper
    mix = jnp.where(pick, acc[:, :width], acc[:, width:])
    out_ref[...] = (mix / whole).astype(out_ref.dtype)
    for copy in sent + swapped:
        copy.wait_send()


def shards(queries, keys, values, stretch_order):
    tokens, heads, width = queries.shape
    rows = tokens * heads
    blocks = lax.axis_size("ctx")
    vmem = pl.BlockSpec(memory_space=pltpu.VMEM)
    out = pl.pallas_call(
        kernel,
        out_shape=jax.ShapeDtypeStruct((rows, width), queries.dtype),
        in_specs=[
            pl.BlockSpec(memory_space=pl.ANY), vmem, vmem,
            pl.BlockSpec(memory_space=pltpu.SMEM),
        ],
        out_specs=vmem,
        scratch_shapes=[
            pltpu.VMEM((rows, width), jnp.bfloat16),
            pltpu.VMEM((rows, 2 * width), jnp.bfloat16),
            pltpu.VMEM((blocks, tokens, width), jnp.bfloat16),
            pltpu.VMEM((blocks, tokens, width), jnp.bfloat16),
            pltpu.VMEM((2, blocks // 4, 4 * tokens), jnp.float32),
            pltpu.VMEM((rows, tokens), jnp.float32),
            pltpu.VMEM((rows, tokens), jnp.float32),
            pltpu.VMEM((rows, 2 * width), jnp.float32),
            pltpu.SemaphoreType.DMA,
            pltpu.SemaphoreType.DMA((SENDS,)),
            pltpu.SemaphoreType.DMA((blocks,)),
            pltpu.SemaphoreType.DMA((SWAPS,)),
            pltpu.SemaphoreType.DMA((SWAPS,)),
        ],
        compiler_params=pltpu.CompilerParams(
            collective_id=0, has_side_effects=True, vmem_limit_bytes=48 * 1024 * 1024
        ),
    )(queries.reshape(rows, width), keys, values, stretch_order)
    return out.reshape(tokens, heads, width)


def solution(mesh):
    in_specs = (P("ctx", "head", None), P("ctx", "head"), P("ctx", "head"), P())
    out_specs = P("ctx", "head", None)
    return jax.shard_map(shards, mesh=mesh, in_specs=in_specs, out_specs=out_specs, check_vma=False)
```

```python
import math

import jax
import jax.numpy as jnp
from jax import lax
from jax.experimental import pallas as pl
from jax.experimental.pallas import tpu as pltpu
from jax.sharding import PartitionSpec as P

MESH = pl.DeviceIdType.MESH
NEG = -1e30


def send(s, *jumps):
    return [("send", s, k) for k in jumps]


def swap(first, count):
    return [("swap", first, count)]


def attend(g):
    return [("attend", 4 * g)]


PROGRAM = (
    send(0, 16, 12, 8, 4, 1, 3, 2, 5, 7, 6)
    + send(8, 1, 3, 2) + send(12, 1, 3, 2) + swap(0, 4)
    + send(16, 12, 8, 4, 1, 3, 2, 5, 7, 6)
    + attend(0)
    + swap(4, 4) + attend(1) + swap(8, 8) + attend(2) + attend(3)
    + send(24, 1, 3, 2) + send(28, 1, 3, 2)
    + swap(16, 8) + attend(4) + attend(5)
    + swap(24, 4) + attend(6) + swap(28, 4) + attend(7)
)
SENDS = sum(op[0] == "send" for op in PROGRAM)
SWAPS = sum(op[0] == "swap" for op in PROGRAM)
GROUP = 4


def kernel(
    q_hbm, k_hbm, v_hbm, table_hbm, out_ref,
    q, kv, table, top, acc,
    in_sem, send_sem, recv_sem, swap_send, swap_recv,
):
    h = lax.axis_index("head")
    c = lax.axis_index("ctx")
    core = h % 2
    half = k_hbm.shape[0]
    tokens = k_hbm.shape[1]
    width = 2 * half
    rows = q.shape[0]
    heads = rows // tokens
    stretch = tokens // 2
    factor = width ** (-0.5) * math.log2(math.e)

    own = [
        pltpu.make_async_copy(k_hbm, kv.at[core, 0, pl.ds(0, half)], in_sem.at[0]),
        pltpu.make_async_copy(v_hbm, kv.at[core, 0, pl.ds(half, half)], in_sem.at[1]),
    ]
    later = [
        pltpu.make_async_copy(table_hbm, table, in_sem.at[2]),
        pltpu.make_async_copy(q_hbm, q, in_sem.at[3]),
    ]
    for copy in own + later:
        copy.start()
    jumps = sorted({op[2] for op in PROGRAM if op[0] == "send"}, reverse=True)
    barrier = pltpu.get_barrier_semaphore()
    for k in jumps:
        pl.semaphore_signal(barrier, inc=1, device_id=(h, c ^ k), device_id_type=MESH)
    pl.semaphore_signal(barrier, inc=1, device_id=(h ^ 1, c), device_id_type=MESH)
    for copy in own:
        copy.wait()
    pl.semaphore_wait(barrier, len(jumps) + 1)

    def remote(s, k, i):
        return pltpu.make_async_remote_copy(
            src_ref=kv.at[core, s], dst_ref=kv.at[core, s ^ k],
            send_sem=send_sem.at[i], recv_sem=recv_sem.at[s ^ k],
            device_id=(h, c ^ k), device_id_type=MESH,
        )

    def across(s, n, i, side):
        part = kv.at[side, pl.ds(s, n)]
        return pltpu.make_async_remote_copy(
            src_ref=part, dst_ref=part,
            send_sem=swap_send.at[i], recv_sem=swap_recv.at[i],
            device_id=(h ^ 1, c), device_id_type=MESH,
        )

    def lift(s, i, a):
        return jnp.where(table[i, c ^ s] < table[a, c], jnp.float32(0), jnp.float32(NEG))

    def step(s0):
        slots = range(s0, s0 + GROUP)
        k_t = jnp.concatenate(
            [jnp.concatenate([kv[0, s, :half], kv[1, s, :half]], axis=0) for s in slots], axis=1
        )
        v_t = jnp.concatenate(
            [jnp.concatenate([kv[0, s, half:], kv[1, s, half:]], axis=0) for s in slots], axis=1
        )
        v_t = jnp.concatenate([v_t, jnp.ones((16, v_t.shape[1]), v_t.dtype)], axis=0)
        spans = [slice(a * rows // 2, (a + 1) * rows // 2) for a in range(2)]
        scores = [
            lax.dot_general(
                k_t, q[span, :], (((0,), (1,)), ((), ())), preferred_element_type=jnp.float32
            )
            for span in spans
        ]
        for a, span in enumerate(spans):
            tiles, lifts = [], []
            for n, s in enumerate(slots):
                for i in range(2):
                    at = n * tokens + i * stretch
                    tile = scores[a][at : at + stretch]
                    if s == 0 and i == a:
                        key = lax.broadcasted_iota(jnp.int32, tile.shape, 0)
                        query = lax.broadcasted_iota(jnp.int32, tile.shape, 1) // heads
                        tile = jnp.where(key <= query, tile, NEG)
                        lifts.append(None)
                    else:
                        lifts.append(lift(s, i, a))
                    tiles.append(tile)
            best = None
            for tile, up in zip(tiles, lifts):
                peak = jnp.max(tile.reshape(stretch // 8, 8, rows // 2), axis=0)
                if up is not None:
                    peak = peak + up
                best = peak if best is None else jnp.maximum(best, peak)
            best = jnp.max(best, axis=0, keepdims=True)
            if s0 != 0:
                old = top[0:1, span]
                best = jnp.maximum(old, best)
            weights = [
                jnp.exp2((tile - (best if up is None else best - up)) * factor).astype(kv.dtype)
                for tile, up in zip(tiles, lifts)
            ]
            mixed = jnp.dot(
                v_t, jnp.concatenate(weights, axis=0), preferred_element_type=jnp.float32
            )
            if s0 != 0:
                mixed = acc[:, span] * jnp.exp2((old - best) * factor) + mixed
            acc[:, span] = mixed
            top[0:1, span] = best

    here = {0}

    def arrived(s):
        if s not in here:
            here.add(s)
            remote(s ^ 1, 1, 0).wait_recv()

    sent, swapped, swap_of, pending = [], [], {}, list(later)
    for op in PROGRAM:
        if op[0] == "send":
            arrived(op[1])
            sent.append(remote(op[1], op[2], len(sent)))
            sent[-1].start()
        elif op[0] == "swap":
            for s in range(op[1], op[1] + op[2]):
                arrived(s)
                swap_of[s] = len(swapped)
            swapped.append((op[1], op[2], len(swapped)))
            across(*swapped[-1], core).start()
        else:
            while pending:
                pending.pop().wait()
            i = swap_of[op[1]]
            if i is not None:
                across(*swapped[i], 1 - core).wait_recv()
                for s in swap_of:
                    if swap_of[s] == i:
                        swap_of[s] = None
            step(op[1])

    mix = acc[:width, :] / acc[width : width + 1, :]
    out_ref[...] = mix.T.astype(out_ref.dtype)
    for copy in sent:
        copy.wait_send()
    for part in swapped:
        across(*part, core).wait_send()


def shards(queries, keys, values, stretch_order):
    tokens, heads, width = queries.shape
    rows = tokens * heads
    blocks = lax.axis_size("ctx")
    out = pl.pallas_call(
        kernel,
        out_shape=jax.ShapeDtypeStruct((rows, width), queries.dtype),
        in_specs=[pl.BlockSpec(memory_space=pltpu.HBM)] * 4,
        out_specs=pl.BlockSpec(memory_space=pltpu.VMEM),
        scratch_shapes=[
            pltpu.VMEM((rows, width), queries.dtype),
            pltpu.VMEM((2, blocks, tokens, width), keys.dtype),
            pltpu.SMEM((2, blocks), jnp.int32),
            pltpu.VMEM((8, rows), jnp.float32),
            pltpu.VMEM((width + 16, rows), jnp.float32),
            pltpu.SemaphoreType.DMA((4,)),
            pltpu.SemaphoreType.DMA((SENDS,)),
            pltpu.SemaphoreType.DMA((blocks,)),
            pltpu.SemaphoreType.DMA((SWAPS,)),
            pltpu.SemaphoreType.DMA((SWAPS,)),
        ],
        compiler_params=pltpu.CompilerParams(
            collective_id=0, has_side_effects=True, vmem_limit_bytes=56 * 1024 * 1024
        ),
    )(queries.reshape(rows, width), keys.T, values.T, stretch_order.T)
    return out.reshape(tokens, heads, width)


def solution(mesh):
    in_specs = (P("ctx", "head", None), P("ctx", "head"), P("ctx", "head"), P())
    out_specs = P("ctx", "head", None)
    return jax.shard_map(shards, mesh=mesh, in_specs=in_specs, out_specs=out_specs, check_vma=False)
```

```python
import math

import jax
import jax.numpy as jnp
from jax import lax
from jax.experimental import pallas as pl
from jax.experimental.pallas import tpu as pltpu
from jax.sharding import PartitionSpec as P

MESH = pl.DeviceIdType.MESH
NEG = -1e30


def send(s, *jumps):
    return [("send", s, k) for k in jumps]


def swap(first, count):
    return [("swap", first, count)]


def attend(g):
    return [("attend", 4 * g)]


FAR = 16
LATE, EVEN, EARLY = range(3)
PROGRAM = (
    [("far", LATE), ("near",)]
    + send(0, 12, 8, 4, 1, 3, 2, 5, 7, 6)
    + [("far", EVEN)]
    + send(8, 1, 3, 2) + send(12, 1, 3, 2)
    + [("far", EARLY)]
    + send(16, 12, 8, 4, 1, 3, 2, 5, 7, 6)
    + swap(0, 4) + attend(0) + swap(4, 4) + attend(1)
    + swap(8, 8) + attend(2)
    + send(24, 1, 3, 2) + attend(3) + send(28, 1, 3, 2)
    + swap(16, 8) + attend(4) + attend(5)
    + swap(24, 4) + attend(6) + swap(28, 4) + attend(7)
)
SENDS = sum(op[0] == "send" for op in PROGRAM)
SWAPS = sum(op[0] == "swap" for op in PROGRAM)
GROUP = 4


def kernel(
    q_hbm, k_hbm, v_hbm, table_hbm, out_ref,
    q, kv, table, top, acc,
    in_sem, send_sem, recv_sem, swap_send, swap_recv, relay,
):
    h = lax.axis_index("head")
    c = lax.axis_index("ctx")
    core = h % 2
    half = k_hbm.shape[0]
    tokens = k_hbm.shape[1]
    width = 2 * half
    rows = q.shape[0]
    heads = rows // tokens
    stretch = tokens // 2
    factor = width ** (-0.5) * math.log2(math.e)

    own = [
        pltpu.make_async_copy(k_hbm, kv.at[core, 0, pl.ds(0, half)], in_sem.at[0]),
        pltpu.make_async_copy(v_hbm, kv.at[core, 0, pl.ds(half, half)], in_sem.at[1]),
    ]
    later = [
        pltpu.make_async_copy(table_hbm, table, in_sem.at[2]),
        pltpu.make_async_copy(q_hbm, q, in_sem.at[3]),
    ]
    for copy in own + later:
        copy.start()
    jumps = sorted({op[2] for op in PROGRAM if op[0] == "send"}, reverse=True)
    barrier = pltpu.get_barrier_semaphore()

    def enter(head, ctx):
        pl.semaphore_signal(barrier, inc=1, device_id=(head, ctx), device_id_type=MESH)

    enter(h - core, c ^ FAR)
    for k in jumps:
        enter(h - core + 1, c ^ k)
    enter(h ^ 1, c)

    def entered(counts, n):
        @pl.when(counts)
        def _():
            pl.semaphore_wait(barrier, n + 1)
            pl.semaphore_signal(relay, inc=1, device_id=(h ^ 1, c), device_id_type=MESH)

        @pl.when(jnp.logical_not(counts))
        def _():
            pl.semaphore_wait(relay, 1)

    for copy in own:
        copy.wait()
    upper_half = c >= FAR
    first_half = h < 8
    stands = {
        LATE: jnp.logical_and(first_half, upper_half),
        EVEN: jnp.logical_not(first_half),
        EARLY: jnp.logical_and(first_half, jnp.logical_not(upper_half)),
    }

    def remote(s, k, i):
        return pltpu.make_async_remote_copy(
            src_ref=kv.at[core, s], dst_ref=kv.at[core, s ^ k],
            send_sem=send_sem.at[i], recv_sem=recv_sem.at[s ^ k],
            device_id=(h, c ^ k), device_id_type=MESH,
        )

    def across(s, n, i, side):
        part = kv.at[side, pl.ds(s, n)]
        return pltpu.make_async_remote_copy(
            src_ref=part, dst_ref=part,
            send_sem=swap_send.at[i], recv_sem=swap_recv.at[i],
            device_id=(h ^ 1, c), device_id_type=MESH,
        )

    def lift(s, i, a):
        return jnp.where(table[i, c ^ s] < table[a, c], jnp.float32(0), jnp.float32(NEG))

    def step(s0):
        slots = range(s0, s0 + GROUP)
        k_t = jnp.concatenate(
            [jnp.concatenate([kv[0, s, :half], kv[1, s, :half]], axis=0) for s in slots], axis=1
        )
        v_t = jnp.concatenate(
            [jnp.concatenate([kv[0, s, half:], kv[1, s, half:]], axis=0) for s in slots], axis=1
        )
        v_t = jnp.concatenate([v_t, jnp.ones((16, v_t.shape[1]), v_t.dtype)], axis=0)
        spans = [slice(a * rows // 2, (a + 1) * rows // 2) for a in range(2)]
        scores = [
            lax.dot_general(
                k_t, q[span, :], (((0,), (1,)), ((), ())), preferred_element_type=jnp.float32
            )
            for span in spans
        ]
        for a, span in enumerate(spans):
            tiles, lifts = [], []
            for n, s in enumerate(slots):
                for i in range(2):
                    at = n * tokens + i * stretch
                    tile = scores[a][at : at + stretch]
                    if s == 0 and i == a:
                        key = lax.broadcasted_iota(jnp.int32, tile.shape, 0)
                        query = lax.broadcasted_iota(jnp.int32, tile.shape, 1) // heads
                        tile = jnp.where(key <= query, tile, NEG)
                        lifts.append(None)
                    else:
                        lifts.append(lift(s, i, a))
                    tiles.append(tile)
            best = None
            for tile, up in zip(tiles, lifts):
                peak = jnp.max(tile.reshape(stretch // 8, 8, rows // 2), axis=0)
                if up is not None:
                    peak = peak + up
                best = peak if best is None else jnp.maximum(best, peak)
            best = jnp.max(best, axis=0, keepdims=True)
            if s0 != 0:
                old = top[0:1, span]
                best = jnp.maximum(old, best)
            weights = [
                jnp.exp2((tile - (best if up is None else best - up)) * factor).astype(kv.dtype)
                for tile, up in zip(tiles, lifts)
            ]
            mixed = jnp.dot(
                v_t, jnp.concatenate(weights, axis=0), preferred_element_type=jnp.float32
            )
            if s0 != 0:
                mixed = acc[:, span] * jnp.exp2((old - best) * factor) + mixed
            acc[:, span] = mixed
            top[0:1, span] = best

    here = {0}

    def arrived(s):
        if s not in here:
            here.add(s)
            remote(s ^ 1, 1, 0).wait_recv()

    sent, swapped, swap_of, pending = [], [], {}, list(later)
    for op in PROGRAM:
        if op[0] == "near":
            entered(core == 1, 2 * len(jumps))
        elif op[0] == "far":

            @pl.when(stands[op[1]])
            def _():
                entered(core == 0, 2)
                remote(0, FAR, SENDS).start()

        elif op[0] == "send":
            arrived(op[1])
            sent.append(remote(op[1], op[2], len(sent)))
            sent[-1].start()
        elif op[0] == "swap":
            for s in range(op[1], op[1] + op[2]):
                arrived(s)
                swap_of[s] = len(swapped)
            swapped.append((op[1], op[2], len(swapped)))
            across(*swapped[-1], core).start()
        else:
            while pending:
                pending.pop().wait()
            i = swap_of[op[1]]
            if i is not None:
                across(*swapped[i], 1 - core).wait_recv()
                for s in swap_of:
                    if swap_of[s] == i:
                        swap_of[s] = None
            step(op[1])

    mix = acc[:width, :] / acc[width : width + 1, :]
    out_ref[...] = mix.T.astype(out_ref.dtype)
    remote(0, FAR, SENDS).wait_send()
    for copy in sent:
        copy.wait_send()
    for part in swapped:
        across(*part, core).wait_send()


def shards(queries, keys, values, stretch_order):
    tokens, heads, width = queries.shape
    rows = tokens * heads
    blocks = lax.axis_size("ctx")
    arrays = (queries.reshape(rows, width), keys.T, values.T, stretch_order.T)
    out = pl.pallas_call(
        kernel,
        out_shape=jax.ShapeDtypeStruct((rows, width), queries.dtype),
        in_specs=[pl.BlockSpec(memory_space=pltpu.HBM)] * 4,
        out_specs=pl.BlockSpec(memory_space=pltpu.VMEM),
        scratch_shapes=[
            pltpu.VMEM((rows, width), queries.dtype),
            pltpu.VMEM((2, blocks, tokens, width), keys.dtype),
            pltpu.SMEM((2, blocks), jnp.int32),
            pltpu.VMEM((8, rows), jnp.float32),
            pltpu.VMEM((width + 16, rows), jnp.float32),
            pltpu.SemaphoreType.DMA((4,)),
            pltpu.SemaphoreType.DMA((SENDS + 1,)),
            pltpu.SemaphoreType.DMA((blocks,)),
            pltpu.SemaphoreType.DMA((SWAPS,)),
            pltpu.SemaphoreType.DMA((SWAPS,)),
            pltpu.SemaphoreType.REGULAR,
        ],
        compiler_params=pltpu.CompilerParams(
            collective_id=0, has_side_effects=True, vmem_limit_bytes=48 * 1024 * 1024
        ),
    )(*(pltpu.with_memory_space_constraint(x, pltpu.HBM) for x in arrays))
    return out.reshape(tokens, heads, width)


def solution(mesh):
    in_specs = (P("ctx", "head", None), P("ctx", "head"), P("ctx", "head"), P())
    out_specs = P("ctx", "head", None)
    return jax.shard_map(shards, mesh=mesh, in_specs=in_specs, out_specs=out_specs, check_vma=False)
```

```python
import math

import jax
import jax.numpy as jnp
from jax import lax
from jax.experimental import pallas as pl
from jax.experimental.pallas import tpu as pltpu
from jax.sharding import PartitionSpec as P

MESH = pl.DeviceIdType.MESH
NEG = -1e30


FAR = 16
LATE, EVEN, EARLY = range(3)
PROGRAM = (
    ("far", LATE), ("near",), ("send", 0, 12), ("send", 0, 1), ("send", 0, 3), ("send", 0, 8),
    ("far", EVEN), ("send", 0, 2), ("far", EARLY), ("send", 3, 4), ("send", 8, 2), ("send", 8, 3),
    ("send", 8, 1), ("swap", 0, 3), ("send", 12, 2), ("send", 12, 1), ("send", 12, 8),
    ("send", 16, 8), ("send", 16, 4), ("send", 16, 3), ("send", 16, 2), ("send", 1, 4),
    ("send", 16, 13), ("send", 16, 1), ("send", 12, 3), ("send", 2, 4), ("swap", 3, 1),
    ("send", 20, 8), ("send", 20, 2), ("send", 20, 3), ("swap", 19, 2), ("send", 19, 12),
    ("send", 20, 1), ("send", 24, 3), ("send", 24, 2), ("send", 18, 12), ("swap", 11, 5),
    ("send", 24, 1), ("swap", 16, 3), ("swap", 4, 5), ("swap", 10, 1), ("attend", (1, 3, 0, 2)),
    ("swap", 9, 1), ("attend", (15, 16, 14, 20)), ("attend", (7, 12, 5, 4)), ("swap", 21, 4),
    ("attend", (6, 19, 18, 10)), ("swap", 28, 2), ("attend", (13, 9, 11, 8)), ("swap", 25, 3),
    ("attend", (22, 23, 17, 24)), ("swap", 30, 2), ("attend", (26, 25, 29, 28)),
    ("attend", (30, 21, 27, 31)),
)
SENDS = sum(op[0] == "send" for op in PROGRAM)
SWAPS = sum(op[0] == "swap" for op in PROGRAM)


def kernel(
    q_hbm, k_hbm, v_hbm, table_hbm, out_ref,
    q, kv, table, top, acc,
    in_sem, send_sem, recv_sem, swap_send, swap_recv, relay,
):
    h = lax.axis_index("head")
    c = lax.axis_index("ctx")
    core = h % 2
    half = k_hbm.shape[0]
    tokens = k_hbm.shape[1]
    width = 2 * half
    rows = q.shape[0]
    heads = rows // tokens
    stretch = tokens // 2
    factor = width ** (-0.5) * math.log2(math.e)

    own = [
        pltpu.make_async_copy(k_hbm, kv.at[core, 0, pl.ds(0, half)], in_sem.at[0]),
        pltpu.make_async_copy(v_hbm, kv.at[core, 0, pl.ds(half, half)], in_sem.at[1]),
    ]
    later = [
        pltpu.make_async_copy(table_hbm, table, in_sem.at[2]),
        pltpu.make_async_copy(q_hbm, q, in_sem.at[3]),
    ]
    for copy in own + later:
        copy.start()
    jumps = sorted({op[2] for op in PROGRAM if op[0] == "send"}, reverse=True)
    barrier = pltpu.get_barrier_semaphore()

    def enter(head, ctx):
        pl.semaphore_signal(barrier, inc=1, device_id=(head, ctx), device_id_type=MESH)

    enter(h - core, c ^ FAR)
    for k in jumps:
        enter(h - core + 1, c ^ k)
    enter(h ^ 1, c)

    def entered(counts, n):
        @pl.when(counts)
        def _():
            pl.semaphore_wait(barrier, n + 1)
            pl.semaphore_signal(relay, inc=1, device_id=(h ^ 1, c), device_id_type=MESH)

        @pl.when(jnp.logical_not(counts))
        def _():
            pl.semaphore_wait(relay, 1)

    for copy in own:
        copy.wait()
    upper_half = c >= FAR
    first_half = h < 8
    stands = {
        LATE: jnp.logical_and(first_half, upper_half),
        EVEN: jnp.logical_not(first_half),
        EARLY: jnp.logical_and(first_half, jnp.logical_not(upper_half)),
    }

    def remote(s, k, i):
        return pltpu.make_async_remote_copy(
            src_ref=kv.at[core, s], dst_ref=kv.at[core, s ^ k],
            send_sem=send_sem.at[i], recv_sem=recv_sem.at[s ^ k],
            device_id=(h, c ^ k), device_id_type=MESH,
        )

    def across(s, n, i, side):
        part = kv.at[side, pl.ds(s, n)]
        return pltpu.make_async_remote_copy(
            src_ref=part, dst_ref=part,
            send_sem=swap_send.at[i], recv_sem=swap_recv.at[i],
            device_id=(h ^ 1, c), device_id_type=MESH,
        )

    def lift(s, i, a):
        return jnp.where(table[i, c ^ s] < table[a, c], jnp.float32(0), jnp.float32(NEG))

    def step(slots, first):
        k_t = jnp.concatenate(
            [jnp.concatenate([kv[0, s, :half], kv[1, s, :half]], axis=0) for s in slots], axis=1
        )
        v_t = jnp.concatenate(
            [jnp.concatenate([kv[0, s, half:], kv[1, s, half:]], axis=0) for s in slots], axis=1
        )
        v_t = jnp.concatenate([v_t, jnp.ones((16, v_t.shape[1]), v_t.dtype)], axis=0)
        spans = [slice(a * rows // 2, (a + 1) * rows // 2) for a in range(2)]
        scores = [
            lax.dot_general(
                k_t, q[span, :], (((0,), (1,)), ((), ())), preferred_element_type=jnp.float32
            )
            for span in spans
        ]
        for a, span in enumerate(spans):
            tiles, lifts = [], []
            for n, s in enumerate(slots):
                for i in range(2):
                    at = n * tokens + i * stretch
                    tile = scores[a][at : at + stretch]
                    if s == 0 and i == a:
                        key = lax.broadcasted_iota(jnp.int32, tile.shape, 0)
                        query = lax.broadcasted_iota(jnp.int32, tile.shape, 1) // heads
                        tile = jnp.where(key <= query, tile, NEG)
                        lifts.append(None)
                    else:
                        lifts.append(lift(s, i, a))
                    tiles.append(tile)
            best = None
            for tile, up in zip(tiles, lifts):
                peak = jnp.max(tile.reshape(stretch // 8, 8, rows // 2), axis=0)
                if up is not None:
                    peak = peak + up
                best = peak if best is None else jnp.maximum(best, peak)
            best = jnp.max(best, axis=0, keepdims=True)
            if not first:
                old = top[0:1, span]
                best = jnp.maximum(old, best)
            weights = [
                jnp.exp2((tile - (best if up is None else best - up)) * factor).astype(kv.dtype)
                for tile, up in zip(tiles, lifts)
            ]
            mixed = jnp.dot(
                v_t, jnp.concatenate(weights, axis=0), preferred_element_type=jnp.float32
            )
            if not first:
                mixed = acc[:, span] * jnp.exp2((old - best) * factor) + mixed
            acc[:, span] = mixed
            top[0:1, span] = best

    here = {0}

    def arrived(s):
        if s not in here:
            here.add(s)
            remote(s ^ 1, 1, 0).wait_recv()

    sent, swapped, swap_of, pending = [], [], {}, list(later)
    crossed, attended = set(), ()
    for op in PROGRAM:
        if op[0] == "near":
            entered(core == 1, 2 * len(jumps))
        elif op[0] == "far":

            @pl.when(stands[op[1]])
            def _():
                entered(core == 0, 2)
                remote(0, FAR, SENDS).start()

        elif op[0] == "send":
            arrived(op[1])
            sent.append(remote(op[1], op[2], len(sent)))
            sent[-1].start()
        elif op[0] == "swap":
            for s in range(op[1], op[1] + op[2]):
                arrived(s)
                swap_of[s] = len(swapped)
            swapped.append((op[1], op[2], len(swapped)))
            across(*swapped[-1], core).start()
        else:
            while pending:
                pending.pop().wait()
            for s in op[1]:
                if swap_of[s] not in crossed:
                    crossed.add(swap_of[s])
                    across(*swapped[swap_of[s]], 1 - core).wait_recv()
            step(op[1], not attended)
            attended += op[1]

    mix = acc[:width, :] / acc[width : width + 1, :]
    out_ref[...] = mix.T.astype(out_ref.dtype)
    remote(0, FAR, SENDS).wait_send()
    for copy in sent:
        copy.wait_send()
    for part in swapped:
        across(*part, core).wait_send()


def shards(queries, keys, values, stretch_order):
    tokens, heads, width = queries.shape
    rows = tokens * heads
    blocks = lax.axis_size("ctx")
    arrays = (queries.reshape(rows, width), keys.T, values.T, stretch_order.T)
    out = pl.pallas_call(
        kernel,
        out_shape=jax.ShapeDtypeStruct((rows, width), queries.dtype),
        in_specs=[pl.BlockSpec(memory_space=pltpu.HBM)] * 4,
        out_specs=pl.BlockSpec(memory_space=pltpu.VMEM),
        scratch_shapes=[
            pltpu.VMEM((rows, width), queries.dtype),
            pltpu.VMEM((2, blocks, tokens, width), keys.dtype),
            pltpu.SMEM((2, blocks), jnp.int32),
            pltpu.VMEM((8, rows), jnp.float32),
            pltpu.VMEM((width + 16, rows), jnp.float32),
            pltpu.SemaphoreType.DMA((4,)),
            pltpu.SemaphoreType.DMA((SENDS + 1,)),
            pltpu.SemaphoreType.DMA((blocks,)),
            pltpu.SemaphoreType.DMA((SWAPS,)),
            pltpu.SemaphoreType.DMA((SWAPS,)),
            pltpu.SemaphoreType.REGULAR,
        ],
        compiler_params=pltpu.CompilerParams(
            collective_id=0, has_side_effects=True, vmem_limit_bytes=48 * 1024 * 1024
        ),
    )(*(pltpu.with_memory_space_constraint(x, pltpu.HBM) for x in arrays))
    return out.reshape(tokens, heads, width)


def solution(mesh):
    in_specs = (P("ctx", "head", None), P("ctx", "head"), P("ctx", "head"), P())
    out_specs = P("ctx", "head", None)
    return jax.shard_map(shards, mesh=mesh, in_specs=in_specs, out_specs=out_specs, check_vma=False)
```

```python
import math

import jax
import jax.numpy as jnp
from jax import lax
from jax.experimental import pallas as pl
from jax.experimental.pallas import tpu as pltpu
from jax.sharding import PartitionSpec as P

MESH = pl.DeviceIdType.MESH
NEG = -1e30


LATE, EVEN, EARLY = range(3)
FACING = (EARLY, EVEN, LATE)
FAR = 16
ATTEND = (
    (0, 3, 1, 2), (9, 24, 12, 11, 13, 10), (6, 14, 15, 4, 8, 5, 7),
    (20, 19, 18, 17, 29, 23, 21, 16), (25, 28, 27, 22), (30, 31, 26),
)
ORDERS = (
    (
        ("send", 0, 16), ("send", 0, 1), ("send", 0, 8), ("cross", 0, 2), ("send", 0, 2),
        ("send", 0, 3), ("send", 0, 12), ("cross", 0, 1), ("cross", 8, 2), ("send", 8, 3),
        ("cross", 12, 3), ("send", 12, 1), ("send", 12, 3), ("send", 8, 2), ("send", 1, 4),
        ("send", 3, 4), ("send", 16, 8), ("send", 16, 3), ("send", 16, 4), ("send", 8, 1),
        ("send", 16, 2), ("send", 16, 1), ("send", 16, 13), ("swap", 3, 1), ("send", 16, 12),
        ("swap", 0, 1), ("send", 7, 1), ("send", 0, 4), ("cross", 13, 3), ("send", 15, 1),
        ("cross", 20, 3), ("swap", 11, 2), ("swap", 24, 1), ("send", 17, 8), ("swap", 13, 1),
        ("cross", 24, 3), ("send", 24, 3), ("cross", 20, 1), ("send", 19, 4), ("cross", 19, 12),
        ("swap", 8, 2), ("send", 20, 1), ("cross", 19, 5), ("attend", 0), ("send", 28, 3),
        ("cross", 24, 1), ("cross", 24, 2), ("send", 28, 2), ("swap", 4, 4), ("send", 18, 4),
        ("send", 24, 2), ("swap", 16, 5), ("cross", 18, 12), ("attend", 1), ("swap", 28, 2),
        ("attend", 2), ("attend", 3), ("attend", 4), ("attend", 5),
    ),
    (
        ("send", 0, 8), ("cross", 0, 2), ("send", 0, 12), ("send", 0, 3), ("send", 0, 7),
        ("send", 0, 16), ("send", 0, 2), ("send", 0, 1), ("cross", 0, 1), ("send", 8, 2),
        ("cross", 8, 2), ("cross", 8, 1), ("send", 8, 12), ("send", 12, 3), ("send", 2, 4),
        ("send", 12, 1), ("send", 12, 2), ("send", 1, 4), ("send", 8, 3), ("send", 16, 4),
        ("send", 16, 1), ("send", 16, 3), ("send", 16, 8), ("send", 16, 2), ("send", 16, 13),
        ("swap", 0, 1), ("swap", 3, 6), ("send", 10, 3), ("cross", 20, 2), ("send", 20, 2),
        ("send", 20, 1), ("swap", 11, 3), ("send", 20, 8), ("send", 24, 3), ("send", 24, 2),
        ("swap", 24, 1), ("cross", 19, 4), ("cross", 24, 1), ("send", 19, 4), ("cross", 19, 12),
        ("attend", 0), ("swap", 14, 5), ("cross", 24, 2), ("send", 19, 12), ("cross", 29, 3),
        ("send", 24, 1), ("send", 29, 3), ("attend", 1), ("swap", 29, 1), ("swap", 19, 3),
        ("attend", 2), ("swap", 27, 2), ("attend", 3), ("attend", 4), ("attend", 5),
    ),
    (
        ("send", 0, 12), ("send", 0, 8), ("cross", 0, 1), ("send", 0, 3), ("send", 0, 1),
        ("send", 0, 2), ("send", 0, 16), ("send", 3, 4), ("send", 8, 2), ("send", 8, 1),
        ("send", 12, 2), ("send", 12, 1), ("send", 8, 12), ("send", 16, 4), ("send", 16, 3),
        ("swap", 12, 1), ("send", 8, 3), ("send", 16, 8), ("send", 2, 4), ("swap", 2, 2),
        ("send", 16, 2), ("send", 16, 1), ("send", 16, 13), ("send", 12, 3), ("swap", 0, 1),
        ("send", 1, 4), ("send", 20, 3), ("send", 20, 2), ("cross", 20, 3), ("cross", 20, 1),
        ("send", 20, 1), ("send", 19, 12), ("swap", 13, 1), ("cross", 20, 2), ("cross", 24, 1),
        ("cross", 24, 4), ("swap", 9, 3), ("swap", 24, 1), ("send", 24, 3), ("cross", 24, 3),
        ("attend", 0), ("swap", 14, 1), ("send", 24, 4), ("swap", 4, 5), ("cross", 18, 12),
        ("cross", 24, 2), ("swap", 15, 1), ("swap", 18, 3), ("send", 24, 1), ("swap", 16, 2),
        ("send", 18, 12), ("send", 24, 2), ("attend", 1), ("swap", 29, 1), ("attend", 2),
        ("swap", 31, 1), ("attend", 3), ("attend", 4), ("attend", 5),
    ),
)


def jumps(kind, far):
    found = {op[2] for op in ORDERS[kind] if op[0] in ("send", "cross")}
    return sorted((k for k in found if (k >= FAR) == far), reverse=True)


SENDS = max(sum(op[0] == "send" for op in order) for order in ORDERS)
CROSSES = max(sum(op[0] == "cross" for op in order) for order in ORDERS)
SWAPS = max(sum(op[0] == "swap" for op in order) for order in ORDERS)


def kernel(
    q_hbm, k_hbm, v_hbm, table_hbm, out_ref,
    q, kv, table, top, acc,
    in_sem, send_sem, recv_sem, swap_send, swap_recv, cross_send, cross_recv, relay,
):
    h = lax.axis_index("head")
    c = lax.axis_index("ctx")
    core = h % 2
    half = k_hbm.shape[0]
    tokens = k_hbm.shape[1]
    width = 2 * half
    rows = q.shape[0]
    heads = rows // tokens
    stretch = tokens // 2
    factor = width ** (-0.5) * math.log2(math.e)

    own = [
        pltpu.make_async_copy(k_hbm, kv.at[core, 0, pl.ds(0, half)], in_sem.at[0]),
        pltpu.make_async_copy(v_hbm, kv.at[core, 0, pl.ds(half, half)], in_sem.at[1]),
    ]
    later = [
        pltpu.make_async_copy(table_hbm, table, in_sem.at[2]),
        pltpu.make_async_copy(q_hbm, q, in_sem.at[3]),
    ]
    for copy in own + later:
        copy.start()
    upper_half = c >= FAR
    first_half = h < 8
    stands = (
        jnp.logical_and(first_half, upper_half),
        jnp.logical_not(first_half),
        jnp.logical_and(first_half, jnp.logical_not(upper_half)),
    )
    kinds = range(len(stands))

    barrier = pltpu.get_barrier_semaphore()

    def enter(head, ctx):
        pl.semaphore_signal(barrier, inc=1, device_id=(head, ctx), device_id_type=MESH)

    enter(h ^ 1, c)
    for kind in kinds:

        @pl.when(stands[kind])
        def _(kind=kind):
            for k in jumps(FACING[kind], True):
                enter(h - core, c ^ k)
            for k in jumps(kind, False):
                enter(h - core + 1, c ^ k)

    for copy in own:
        copy.wait()

    def entered(kind, far):
        counts = core == (0 if far else 1)

        @pl.when(counts)
        def _():
            pl.semaphore_wait(barrier, 2 * len(jumps(kind, far)) + 1)
            pl.semaphore_signal(relay, inc=1, device_id=(h ^ 1, c), device_id_type=MESH)

        @pl.when(jnp.logical_not(counts))
        def _():
            pl.semaphore_wait(relay, 1)

    def remote(s, k, i):
        return pltpu.make_async_remote_copy(
            src_ref=kv.at[core, s], dst_ref=kv.at[core, s ^ k],
            send_sem=send_sem.at[i], recv_sem=recv_sem.at[s ^ k],
            device_id=(h, c ^ k), device_id_type=MESH,
        )

    def across(s, n, i, side):
        part = kv.at[side, pl.ds(s, n)]
        return pltpu.make_async_remote_copy(
            src_ref=part, dst_ref=part,
            send_sem=swap_send.at[i], recv_sem=swap_recv.at[i],
            device_id=(h ^ 1, c), device_id_type=MESH,
        )

    def lift(s, i, a):
        return jnp.where(table[i, c ^ s] < table[a, c], jnp.float32(0), jnp.float32(NEG))

    def step(slots, first):
        k_t = jnp.concatenate(
            [jnp.concatenate([kv[0, s, :half], kv[1, s, :half]], axis=0) for s in slots], axis=1
        )
        v_t = jnp.concatenate(
            [jnp.concatenate([kv[0, s, half:], kv[1, s, half:]], axis=0) for s in slots], axis=1
        )
        v_t = jnp.concatenate([v_t, jnp.ones((16, v_t.shape[1]), v_t.dtype)], axis=0)
        spans = [slice(a * rows // 2, (a + 1) * rows // 2) for a in range(2)]
        scores = [
            lax.dot_general(
                k_t, q[span, :], (((0,), (1,)), ((), ())), preferred_element_type=jnp.float32
            )
            for span in spans
        ]
        for a, span in enumerate(spans):
            tiles, lifts = [], []
            for n, s in enumerate(slots):
                for i in range(2):
                    at = n * tokens + i * stretch
                    tile = scores[a][at : at + stretch]
                    if s == 0 and i == a:
                        key = lax.broadcasted_iota(jnp.int32, tile.shape, 0)
                        query = lax.broadcasted_iota(jnp.int32, tile.shape, 1) // heads
                        tile = jnp.where(key <= query, tile, NEG)
                        lifts.append(None)
                    else:
                        lifts.append(lift(s, i, a))
                    tiles.append(tile)
            best = None
            for tile, up in zip(tiles, lifts):
                peak = jnp.max(tile.reshape(stretch // 8, 8, rows // 2), axis=0)
                if up is not None:
                    peak = peak + up
                best = peak if best is None else jnp.maximum(best, peak)
            best = jnp.max(best, axis=0, keepdims=True)
            if not first:
                old = top[0:1, span]
                best = jnp.maximum(old, best)
            weights = [
                jnp.exp2((tile - (best if up is None else best - up)) * factor).astype(kv.dtype)
                for tile, up in zip(tiles, lifts)
            ]
            mixed = jnp.dot(
                v_t, jnp.concatenate(weights, axis=0), preferred_element_type=jnp.float32
            )
            if not first:
                mixed = acc[:, span] * jnp.exp2((old - best) * factor) + mixed
            acc[:, span] = mixed
            top[0:1, span] = best

    def over(s, k, i):
        return pltpu.make_async_remote_copy(
            src_ref=kv.at[core, s], dst_ref=kv.at[core, s ^ k],
            send_sem=cross_send.at[i], recv_sem=cross_recv.at[s ^ k],
            device_id=(h ^ 1, c ^ k), device_id_type=MESH,
        )

    def came_over(s):
        part = kv.at[1 - core, s]
        return pltpu.make_async_remote_copy(
            src_ref=part, dst_ref=part,
            send_sem=cross_send.at[0], recv_sem=cross_recv.at[s],
            device_id=(h ^ 1, c), device_id_type=MESH,
        )

    here = [{0} for _ in kinds]
    passed = [[] for _ in kinds]
    known = [set() for _ in kinds]
    sent = [[] for _ in kinds]
    swapped = [[] for _ in kinds]
    crossed = [set() for _ in kinds]

    def arrived(kind, s):
        if s not in here[kind]:
            here[kind].add(s)
            remote(s ^ 1, 1, 0).wait_recv()

    def meet(kind, far):
        if far not in known[kind]:
            known[kind].add(far)
            entered(kind, far)

    def move(kind, ops):
        for op in ops:
            if op[0] == "send":
                meet(kind, op[2] >= FAR)
                arrived(kind, op[1])
                sent[kind].append((op[1], op[2], len(sent[kind])))
                remote(*sent[kind][-1]).start()
            elif op[0] == "cross":
                meet(kind, op[2] >= FAR)
                arrived(kind, op[1])
                passed[kind].append((op[1], op[2], len(passed[kind])))
                over(*passed[kind][-1]).start()
            elif op[0] == "swap":
                if not known[kind]:
                    meet(kind, False)
                for s in range(op[1], op[1] + op[2]):
                    arrived(kind, s)
                swapped[kind].append((op[1], op[2], len(swapped[kind])))
                across(*swapped[kind][-1], core).start()
            else:
                for part in swapped[kind]:
                    reach = set(range(part[0], part[0] + part[1]))
                    if part not in crossed[kind] and reach & set(ATTEND[op[1]]):
                        crossed[kind].add(part)
                        across(*part, 1 - core).wait_recv()
                near = {o[1] ^ o[2] for o in ORDERS[kind] if o[0] == "cross" and o[2] < FAR}
                far = {o[1] ^ o[2] for o in ORDERS[FACING[kind]] if o[0] == "cross" and o[2] >= FAR}
                for s in ATTEND[op[1]]:
                    arrived(kind, s)
                    if s in near | far:
                        came_over(s).wait_recv()

    starts = [0 for _ in kinds]
    for i, slots in enumerate(ATTEND):
        for kind in kinds:
            end = ORDERS[kind].index(("attend", i)) + 1

            @pl.when(stands[kind])
            def _(kind=kind, end=end):
                move(kind, ORDERS[kind][starts[kind] : end])

            starts[kind] = end
        if i == 0:
            for copy in later:
                copy.wait()
        step(slots, i == 0)

    mix = acc[:width, :] * (1.0 / acc[width : width + 1, :])
    out_ref[...] = mix.astype(out_ref.dtype).T
    for kind in kinds:

        @pl.when(stands[kind])
        def _(kind=kind):
            move(kind, ORDERS[kind][starts[kind] :])
            for part in sent[kind]:
                remote(*part).wait_send()
            for part in passed[kind]:
                over(*part).wait_send()
            for part in swapped[kind]:
                across(*part, core).wait_send()


def shards(queries, keys, values, stretch_order):
    tokens, heads, width = queries.shape
    rows = tokens * heads
    blocks = lax.axis_size("ctx")
    arrays = (queries.reshape(rows, width), keys.T, values.T, stretch_order.T)
    out = pl.pallas_call(
        kernel,
        out_shape=jax.ShapeDtypeStruct((rows, width), queries.dtype),
        in_specs=[pl.BlockSpec(memory_space=pltpu.HBM)] * 4,
        out_specs=pl.BlockSpec(memory_space=pltpu.VMEM),
        scratch_shapes=[
            pltpu.VMEM((rows, width), queries.dtype),
            pltpu.VMEM((2, blocks, tokens, width), keys.dtype),
            pltpu.SMEM((2, blocks), jnp.int32),
            pltpu.VMEM((8, rows), jnp.float32),
            pltpu.VMEM((width + 16, rows), jnp.float32),
            pltpu.SemaphoreType.DMA((4,)),
            pltpu.SemaphoreType.DMA((SENDS,)),
            pltpu.SemaphoreType.DMA((blocks,)),
            pltpu.SemaphoreType.DMA((SWAPS,)),
            pltpu.SemaphoreType.DMA((SWAPS,)),
            pltpu.SemaphoreType.DMA((max(CROSSES, 1),)),
            pltpu.SemaphoreType.DMA((blocks,)),
            pltpu.SemaphoreType.REGULAR,
        ],
        compiler_params=pltpu.CompilerParams(
            collective_id=0, has_side_effects=True, vmem_limit_bytes=48 * 1024 * 1024
        ),
    )(*(pltpu.with_memory_space_constraint(x, pltpu.HBM) for x in arrays))
    return out.reshape(tokens, heads, width)


def solution(mesh):
    in_specs = (P("ctx", "head", None), P("ctx", "head"), P("ctx", "head"), P())
    out_specs = P("ctx", "head", None)
    return jax.shard_map(shards, mesh=mesh, in_specs=in_specs, out_specs=out_specs, check_vma=False)
```

```python
import math

import jax
import jax.numpy as jnp
from jax import lax
from jax.experimental import pallas as pl
from jax.experimental.pallas import tpu as pltpu
from jax.sharding import PartitionSpec as P

MESH = pl.DeviceIdType.MESH
NEG = -1e30


FAR = 16
LATE, EVEN, EARLY = range(3)
PROGRAM = (
    ("far", LATE), ("near",), ("send", 0, 12), ("send", 0, 1), ("send", 0, 3), ("send", 0, 8),
    ("far", EVEN), ("send", 0, 2), ("far", EARLY), ("send", 3, 4), ("send", 8, 2), ("send", 8, 3),
    ("send", 8, 1), ("swap", 0, 3), ("send", 12, 2), ("send", 12, 1), ("send", 12, 8),
    ("send", 16, 8), ("send", 16, 4), ("send", 16, 3), ("send", 16, 2), ("send", 1, 4),
    ("send", 16, 13), ("send", 16, 1), ("send", 12, 3), ("send", 2, 4), ("swap", 3, 1),
    ("send", 20, 8), ("send", 20, 2), ("send", 20, 3), ("swap", 19, 2), ("send", 19, 12),
    ("send", 20, 1), ("send", 24, 3), ("send", 24, 2), ("send", 18, 12), ("swap", 11, 5),
    ("send", 24, 1), ("swap", 16, 3), ("swap", 4, 5), ("swap", 10, 1), ("attend", (1, 3, 0, 2)),
    ("swap", 9, 1), ("attend", (15, 16, 14, 20)), ("attend", (7, 12, 5, 4)), ("swap", 21, 4),
    ("attend", (6, 19, 18, 10)), ("swap", 28, 2), ("attend", (13, 9, 11, 8)), ("swap", 25, 3),
    ("attend", (22, 23, 17, 24)), ("swap", 30, 2), ("attend", (26, 25, 29, 28, 21, 27)),
    ("attend", (30, 31)),
)
SENDS = sum(op[0] == "send" for op in PROGRAM)
SWAPS = sum(op[0] == "swap" for op in PROGRAM)


def kernel(
    q_hbm, k_hbm, v_hbm, table_hbm, out_ref,
    q, kv, table, top, acc,
    in_sem, send_sem, recv_sem, swap_send, swap_recv, relay,
):
    h = lax.axis_index("head")
    c = lax.axis_index("ctx")
    core = h % 2
    half = k_hbm.shape[0]
    tokens = k_hbm.shape[1]
    width = 2 * half
    rows = q.shape[0]
    heads = rows // tokens
    stretch = tokens // 2
    factor = width ** (-0.5) * math.log2(math.e)

    own = [
        pltpu.make_async_copy(k_hbm, kv.at[core, 0, pl.ds(0, half)], in_sem.at[0]),
        pltpu.make_async_copy(v_hbm, kv.at[core, 0, pl.ds(half, half)], in_sem.at[1]),
    ]
    later = [
        pltpu.make_async_copy(table_hbm, table, in_sem.at[2]),
        pltpu.make_async_copy(q_hbm, q, in_sem.at[3]),
    ]
    for copy in own + later:
        copy.start()
    jumps = sorted({op[2] for op in PROGRAM if op[0] == "send"}, reverse=True)
    barrier = pltpu.get_barrier_semaphore()

    def enter(head, ctx):
        pl.semaphore_signal(barrier, inc=1, device_id=(head, ctx), device_id_type=MESH)

    enter(h - core, c ^ FAR)
    for k in jumps:
        enter(h - core + 1, c ^ k)
    enter(h ^ 1, c)

    def entered(counts, n):
        @pl.when(counts)
        def _():
            pl.semaphore_wait(barrier, n + 1)
            pl.semaphore_signal(relay, inc=1, device_id=(h ^ 1, c), device_id_type=MESH)

        @pl.when(jnp.logical_not(counts))
        def _():
            pl.semaphore_wait(relay, 1)

    for copy in own:
        copy.wait()
    upper_half = c >= FAR
    first_half = h < 8
    stands = {
        LATE: jnp.logical_and(first_half, upper_half),
        EVEN: jnp.logical_not(first_half),
        EARLY: jnp.logical_and(first_half, jnp.logical_not(upper_half)),
    }

    def remote(s, k, i):
        return pltpu.make_async_remote_copy(
            src_ref=kv.at[core, s], dst_ref=kv.at[core, s ^ k],
            send_sem=send_sem.at[i], recv_sem=recv_sem.at[s ^ k],
            device_id=(h, c ^ k), device_id_type=MESH,
        )

    def across(s, n, i, side):
        part = kv.at[side, pl.ds(s, n)]
        return pltpu.make_async_remote_copy(
            src_ref=part, dst_ref=part,
            send_sem=swap_send.at[i], recv_sem=swap_recv.at[i],
            device_id=(h ^ 1, c), device_id_type=MESH,
        )

    def lift(s, i, a):
        return jnp.where(table[i, c ^ s] < table[a, c], jnp.float32(0), jnp.float32(NEG))

    def step(slots, first):
        k_t = jnp.concatenate(
            [jnp.concatenate([kv[0, s, :half], kv[1, s, :half]], axis=0) for s in slots], axis=1
        )
        v_t = jnp.concatenate(
            [jnp.concatenate([kv[0, s, half:], kv[1, s, half:]], axis=0) for s in slots], axis=1
        )
        v_t = jnp.concatenate([v_t, jnp.ones((16, v_t.shape[1]), v_t.dtype)], axis=0)
        spans = [slice(a * rows // 2, (a + 1) * rows // 2) for a in range(2)]
        scores = [
            lax.dot_general(
                k_t, q[span, :], (((0,), (1,)), ((), ())), preferred_element_type=jnp.float32
            )
            for span in spans
        ]
        for a, span in enumerate(spans):
            tiles, lifts = [], []
            for n, s in enumerate(slots):
                for i in range(2):
                    at = n * tokens + i * stretch
                    tile = scores[a][at : at + stretch]
                    if s == 0 and i == a:
                        key = lax.broadcasted_iota(jnp.int32, tile.shape, 0)
                        query = lax.broadcasted_iota(jnp.int32, tile.shape, 1) // heads
                        tile = jnp.where(key <= query, tile, NEG)
                        lifts.append(None)
                    else:
                        lifts.append(lift(s, i, a))
                    tiles.append(tile)
            best = None
            for tile, up in zip(tiles, lifts):
                peak = jnp.max(tile.reshape(stretch // 8, 8, rows // 2), axis=0)
                if up is not None:
                    peak = peak + up
                best = peak if best is None else jnp.maximum(best, peak)
            best = jnp.max(best, axis=0, keepdims=True)
            if not first:
                old = top[0:1, span]
                best = jnp.maximum(old, best)
            weights = [
                jnp.exp2((tile - (best if up is None else best - up)) * factor).astype(kv.dtype)
                for tile, up in zip(tiles, lifts)
            ]
            mixed = jnp.dot(
                v_t, jnp.concatenate(weights, axis=0), preferred_element_type=jnp.float32
            )
            if not first:
                mixed = acc[:, span] * jnp.exp2((old - best) * factor) + mixed
            acc[:, span] = mixed
            top[0:1, span] = best

    here = {0}

    def arrived(s):
        if s not in here:
            here.add(s)
            remote(s ^ 1, 1, 0).wait_recv()

    sent, swapped, swap_of, pending = [], [], {}, list(later)
    crossed, attended = set(), ()
    for op in PROGRAM:
        if op[0] == "near":
            entered(core == 1, 2 * len(jumps))
        elif op[0] == "far":

            @pl.when(stands[op[1]])
            def _():
                entered(core == 0, 2)
                remote(0, FAR, SENDS).start()

        elif op[0] == "send":
            arrived(op[1])
            sent.append(remote(op[1], op[2], len(sent)))
            sent[-1].start()
        elif op[0] == "swap":
            for s in range(op[1], op[1] + op[2]):
                arrived(s)
                swap_of[s] = len(swapped)
            swapped.append((op[1], op[2], len(swapped)))
            across(*swapped[-1], core).start()
        else:
            while pending:
                pending.pop().wait()
            for s in op[1]:
                if swap_of[s] not in crossed:
                    crossed.add(swap_of[s])
                    across(*swapped[swap_of[s]], 1 - core).wait_recv()
            step(op[1], not attended)
            attended += op[1]

    mix = acc[:width, :] / acc[width : width + 1, :]
    out_ref[...] = mix.T.astype(out_ref.dtype)
    remote(0, FAR, SENDS).wait_send()
    for copy in sent:
        copy.wait_send()
    for part in swapped:
        across(*part, core).wait_send()


def shards(queries, keys, values, stretch_order):
    tokens, heads, width = queries.shape
    rows = tokens * heads
    blocks = lax.axis_size("ctx")
    arrays = (queries.reshape(rows, width), keys.T, values.T, stretch_order.T)
    out = pl.pallas_call(
        kernel,
        out_shape=jax.ShapeDtypeStruct((rows, width), queries.dtype),
        in_specs=[pl.BlockSpec(memory_space=pltpu.HBM)] * 4,
        out_specs=pl.BlockSpec(memory_space=pltpu.VMEM),
        scratch_shapes=[
            pltpu.VMEM((rows, width), queries.dtype),
            pltpu.VMEM((2, blocks, tokens, width), keys.dtype),
            pltpu.SMEM((2, blocks), jnp.int32),
            pltpu.VMEM((8, rows), jnp.float32),
            pltpu.VMEM((width + 16, rows), jnp.float32),
            pltpu.SemaphoreType.DMA((4,)),
            pltpu.SemaphoreType.DMA((SENDS + 1,)),
            pltpu.SemaphoreType.DMA((blocks,)),
            pltpu.SemaphoreType.DMA((SWAPS,)),
            pltpu.SemaphoreType.DMA((SWAPS,)),
            pltpu.SemaphoreType.REGULAR,
        ],
        compiler_params=pltpu.CompilerParams(
            collective_id=0, has_side_effects=True, vmem_limit_bytes=48 * 1024 * 1024
        ),
    )(*(pltpu.with_memory_space_constraint(x, pltpu.HBM) for x in arrays))
    return out.reshape(tokens, heads, width)


def solution(mesh):
    in_specs = (P("ctx", "head", None), P("ctx", "head"), P("ctx", "head"), P())
    out_specs = P("ctx", "head", None)
    return jax.shard_map(shards, mesh=mesh, in_specs=in_specs, out_specs=out_specs, check_vma=False)
```
